512 devices in a mesh: dp: 16 (over x, y), expert: 32 (over z, core).
Axes of the slice: x: 4, y: 4, z: 16, core: 2. Of those that a mesh axis runs over, the one named last changes fastest.
Arguments:
- tokens: bfloat16 [4096, 4096], P('expert', 'dp'), may hold values from -6 to 6
- expert_ids: int32 [4096, 8], P('expert'), may hold values from 0 to 127, all different within a row; in each aligned block of 128 rows (0 to 127, 128 to 255, ...) at most 12 rows name the same one
- gate_codes: int32 [4096, 8], P('expert'), may hold values from 1 to 255
- out_grad: bfloat16 [4096, 4096], P('expert', 'dp'), may hold values from -3 to 3
- w_in: bfloat16 [32, 4096, 3072], P('expert', 'dp'), may hold values from -0.09375 to 0.09375
- w_out: bfloat16 [32, 1536, 4096], P('expert', None, 'dp'), may hold values from -0.625 to 0.625
Outputs:
- output: bfloat16 [4096, 4096], P('expert', 'dp')
- token_grad: bfloat16 [4096, 4096], P('expert', 'dp')
- w_in_grad: bfloat16 [32, 4096, 3072], P('expert', 'dp')
- w_out_grad: bfloat16 [32, 1536, 4096], P('expert', None, 'dp')
The draws below stay inside these ranges and needn't reach their ends.
Inputs may be any that keep to these rules, and one draw needn't show every extreme that they name: `expert_ids`: each token names 8 different experts. Among the 128 tokens of one index of the expert axis (aligned blocks of tokens) no expert is named by more than 12 tokens, a bound that some block reaches.
All inputs are finite; a program needn't handle non-finite values.
Results may differ from the reference program's by a relative error of at most 0.029.
Values may be sent and summed in bfloat16 or wider, within the bound.
A program may use at most 64 MiB of HBM per device.

```python
import math
import jax
import jax.numpy as jnp
import numpy as np
from jax import lax

D = 4096
FF = 1536
ALL_EXP = 128
TOPK = 8
TOK_DEV = 128
EXPERTS = 32
TOKENS = 4096
CAP = 12
N_DP = 16
N_EXPERT = 32


def place_ends(array, rng, least, top_value):
    longest = array.shape.index(max(array.shape))
    spots = []
    for shift in (0, 1):
        where = [jax.random.randint(jax.random.fold_in(rng, axis), (), 0, length) for axis, length in enumerate(array.shape)]
        where[longest] = (where[longest] + shift) % array.shape[longest]
        spots.append(tuple(where))
    return array.at[spots[0]].set(least).at[spots[1]].set(top_value)


def block_levels(own_key, shape, pieces, least, top_value):
    def one(axis_at, parts):
        heights = jax.random.uniform(jax.random.fold_in(jax.random.fold_in(own_key, 6), axis_at), (parts,), jnp.float32, least / len(pieces), top_value / len(pieces))
        return jnp.repeat(jnp.exp(heights), shape[axis_at] // parts).reshape((-1,) + (1,) * (len(shape) - axis_at - 1))

    level = one(*pieces[0])
    for cut in pieces[1:]:
        level = level * one(*cut)
    return level


def routed_block(key, own, number, rows, amount, top, bound, lean):
    order = jax.random.permutation(key, amount)
    packed, ordinary = load_shares(amount, rows * top, bound, lean, True), load_shares(amount, rows * top, bound, lean, False)
    places = jnp.arange(amount)

    def named(tallies, rotation):
        used = int((tallies > 0).sum())
        fixed = max(1, used // 4)
        passed = fixed + (places - fixed + rotation * (used - fixed)) % max(1, amount - fixed)
        return jnp.zeros((amount,), jnp.int32).at[order[jnp.where(places < fixed, places, passed)]].set(jnp.asarray(tallies, jnp.int32))

    tallies = jnp.where(number % 4 == 0, named(packed, number // 4), named(ordinary, number - number // 4 - 1))
    mixed = jax.random.permutation(jax.random.fold_in(own, 3), amount)
    giver, taker = mixed[0:amount // 2 * 2:2], mixed[1:amount // 2 * 2:2]
    room = jnp.minimum(tallies[giver] - 1, bound - tallies[taker]) // 2
    room = jnp.where((giver == order[0]) | (taker == order[0]) | (tallies[taker] == 0), 0, jnp.maximum(room, 0))
    passed = jax.random.randint(jax.random.fold_in(own, 4), (amount // 2,), 0, 1 << 20) % (room + 1)
    tallies = tallies.at[giver].add(-passed).at[taker].add(passed)
    members = jnp.searchsorted(jnp.cumsum(tallies), jnp.arange(rows * top), side="right").astype(jnp.int32)
    listing = members.reshape(top, rows).T
    listing = listing[jax.random.permutation(jax.random.fold_in(own, 1), rows)]
    rotation = jax.random.randint(jax.random.fold_in(own, 2), (rows, 1), 0, top)
    return jnp.take_along_axis(listing, (jnp.arange(top)[None, :] + rotation) % top, axis=1)


def load_shares(amount, total, most, lean, full):
    portions = [(1 << 20) // math.isqrt(grade ** lean) + 1 for grade in range(1, amount + 1)]
    largest = most if full else min(most, max(-(-total // amount), total * portions[0] // sum(portions)))
    least = 1 if total - largest >= amount - 1 else 0
    given, rest = [largest] + [least] * (amount - 1), total - largest - least * (amount - 1)
    while rest > 0:
        candidates = [i for i in range(1, amount) if given[i] < largest] or [i for i in range(1, amount) if given[i] < most]
        whole, remaining = sum([portions[i] for i in candidates]), rest
        for i in candidates:
            more = min(most - given[i], max(1, remaining * portions[i] // whole), rest)
            given[i] = given[i] + more
            rest = rest - more
    return np.array(given)


def gaussian(own_key, extent, scale, most, pieces=(), kind=jnp.bfloat16):
    entries = jax.random.normal(own_key, extent, jnp.float32) * scale
    if len(pieces) > 0:
        entries = block_levels(own_key, extent, pieces, -0.22, 0.18) * entries
    return jnp.clip(entries, min=-most, max=most).astype(kind)


def setup_inputs(seed: int = 0) -> dict:
    keys = jax.random.split(jax.random.key(seed), 7)
    tokens = gaussian(keys[0], (TOKENS, D), 1.0, 6.0, ((0, 32), (1, 16)))
    expert_ids_keys = jax.random.split(jax.random.fold_in(keys[1], 1), TOKENS // TOK_DEV)
    expert_ids_turns = jax.random.permutation(jax.random.fold_in(keys[1], 3), TOKENS // TOK_DEV)
    expert_ids = jax.vmap(lambda own, number: routed_block(jax.random.fold_in(keys[1], 2), own, number, TOK_DEV, ALL_EXP, TOPK, CAP, 2))(expert_ids_keys, expert_ids_turns).reshape((TOKENS, TOPK))
    gate_codes = place_ends(jax.random.randint(keys[2], (TOKENS, TOPK), 1, 256), jax.random.fold_in(keys[2], 1), 1, 255).astype(jnp.int32)
    out_grad = gaussian(keys[3], (TOKENS, D), 0.5, 3.0, ((0, 32), (1, 16)))
    w_in = gaussian(keys[4], (EXPERTS, D, 2 * FF), D ** -0.5, 0.09375, ((0, 32), (1, 16)))
    w_out = gaussian(keys[5], (EXPERTS, FF, D), (FF // 16) ** -0.5, 0.625, ((0, 32), (2, 16)))
    return dict(tokens=tokens, expert_ids=expert_ids, gate_codes=gate_codes, out_grad=out_grad, w_in=w_in, w_out=w_out)


def activation(values):
    sigma = jax.nn.sigmoid(values)
    return values * sigma, sigma * (1.0 + values * (1.0 - sigma))


def reference(tokens, expert_ids, gate_codes, out_grad, w_in, w_out):
    token_total = tokens.shape[0]
    slice_width = D // N_DP
    rows_total = N_EXPERT * CAP
    code_values = gate_codes.astype(jnp.float32)
    shares = code_values / jnp.sum(code_values, axis=1, keepdims=True)
    token_index = jnp.arange(token_total, dtype=jnp.int32)

    def per_expert(items):
        expert_index, expert_win, expert_wout = items
        hits = expert_ids == expert_index
        chosen = jnp.any(hits, axis=1)
        weight_t = jnp.sum(jnp.where(hits, shares, 0.0), axis=1)
        chosen_blocks = chosen.reshape(N_EXPERT, TOK_DEV).astype(jnp.int32)
        rank = (jnp.cumsum(chosen_blocks, axis=1).astype(jnp.int32) - chosen_blocks).reshape(-1).astype(jnp.int32)
        slot = jnp.where(chosen, (token_index // TOK_DEV) * CAP + rank, rows_total).astype(jnp.int32)
        owner_rows = jnp.zeros((rows_total,), jnp.int32).at[slot].set(token_index, mode="drop")
        present_row = jnp.zeros((rows_total,), jnp.bool_).at[slot].set(True, mode="drop")
        route_weight = jnp.where(present_row, weight_t[owner_rows], 0.0)
        inputs = jnp.where(present_row[:, None], tokens[owner_rows], jnp.zeros((), tokens.dtype))
        route_grads = (route_weight[:, None] * out_grad[owner_rows].astype(jnp.float32)).astype(jnp.bfloat16)
        partial_value = jnp.einsum("mpd,pdf->pmf", inputs.astype(jnp.float32).reshape(rows_total, N_DP, slice_width),
                             expert_win.astype(jnp.float32).reshape(N_DP, slice_width, 2 * FF))
        pre = jnp.sum(lax.optimization_barrier(partial_value.astype(jnp.bfloat16)).astype(jnp.float32), axis=0)
        gate_pre = pre[:, :FF]
        up_pre = pre[:, FF:]
        active, slopes = activation(gate_pre)
        hidden = (active * up_pre).astype(jnp.bfloat16)
        expert_out = jnp.dot(hidden, expert_wout, preferred_element_type=jnp.float32).astype(jnp.bfloat16)
        wout_grad = jnp.dot(hidden.T, route_grads, preferred_element_type=jnp.float32).astype(jnp.bfloat16)
        grad_partial = jnp.einsum("mpd,fpd->pmf", route_grads.astype(jnp.float32).reshape(rows_total, N_DP, slice_width),
                                  expert_wout.astype(jnp.float32).reshape(FF, N_DP, slice_width))
        hidden_grad = jnp.sum(lax.optimization_barrier(grad_partial.astype(jnp.bfloat16)).astype(jnp.float32), axis=0)
        unit_grad = jnp.concatenate([hidden_grad * up_pre * slopes, hidden_grad * active], axis=1).astype(jnp.bfloat16)
        win_grad = jnp.dot(inputs.T, unit_grad, preferred_element_type=jnp.float32).astype(jnp.bfloat16)
        input_grad = jnp.dot(unit_grad, expert_win.T, preferred_element_type=jnp.float32).astype(jnp.bfloat16)
        return expert_out, input_grad, win_grad, wout_grad, owner_rows, route_weight

    expert_range = jnp.arange(EXPERTS, dtype=jnp.int32)
    outs, input_grads, w_in_grad, w_out_grad, owners, weights = lax.map(per_expert, (expert_range, w_in, w_out))
    flat_owner = owners.reshape(-1).astype(jnp.int32)
    output = jnp.zeros((token_total, D), jnp.float32).at[flat_owner].add(
        weights.reshape(-1, 1) * outs.reshape(-1, D).astype(jnp.float32))
    token_grad = jnp.zeros((token_total, D), jnp.float32).at[flat_owner].add(
        input_grads.reshape(-1, D).astype(jnp.float32))
    return output.astype(jnp.bfloat16), token_grad.astype(jnp.bfloat16), w_in_grad, w_out_grad
```

```python
import functools

import jax
import jax.numpy as jnp
from jax import lax
from jax.experimental import pallas as pl
from jax.experimental.pallas import tpu as pltpu
from jax.sharding import PartitionSpec as P

ALL_EXP = 128
SIDE = 4
ROW = 16
MESH = pl.DeviceIdType.MESH
BF = jnp.bfloat16
F32 = jnp.float32


def dot(a, b, ca, cb):
    return lax.dot_general(a, b, (((ca,), (cb,)), ((), ())), preferred_element_type=F32)


def activation(values):
    sigma = jax.nn.sigmoid(values)
    return values * sigma, sigma * (1.0 + values * (1.0 - sigma))


class Ring:
    def __init__(self, place, device_of, send_sems, recv_sems):
        self.place, self.device_of = place, device_of
        self.send_sems, self.recv_sems = send_sems, recv_sems

    def at(self, step):
        return lax.rem(self.place + (step + SIDE), SIDE)

    def copy(self, number, src, dst, step):
        return pltpu.make_async_remote_copy(
            src_ref=src, dst_ref=dst, send_sem=self.send_sems.at[number], recv_sem=self.recv_sems.at[number],
            device_id=self.device_of(self.at(step)), device_id_type=MESH)


class ReduceScatter:
    def __init__(self, ring, block, tmp, summed, arrived, half):
        self.ring, self.block, self.tmp, self.summed = ring, block, tmp, summed
        r = ring
        self.first = (r.copy(0, block(r.at(2), 0), tmp.at[0], 1), r.copy(1, block(r.at(2), 1), tmp.at[1], -1))
        self.second = (r.copy(2, block(r.at(1), 1), half(arrived.at[0], 1), 1),
                       r.copy(3, block(r.at(-1), 0), half(arrived.at[1], 0), -1))
        self.third = (r.copy(4, summed.at[0], half(arrived.at[0], 0), 1),
                      r.copy(5, summed.at[1], half(arrived.at[1], 1), -1))

    def start(self):
        for c in self.first + self.second:
            c.start()

    def relay(self):
        for way, (step, h) in enumerate(((1, 0), (-1, 1))):
            self.first[way].wait_recv()
            mine = self.block(self.ring.at(step), h)[...]
            self.summed[way] = (mine.astype(F32) + self.tmp[way].astype(F32)).astype(BF)
            self.third[way].start()

    def wait(self):
        for c in self.second + self.third:
            c.wait_recv()

    def drain(self):
        for c in self.first + self.second + self.third:
            c.wait_send()


class AllGather:
    def __init__(self, ring, region):
        r = ring
        send = lambda number, q, h, step: r.copy(number, region(q, h), region(q, h), step)
        own, left, right = r.at(0), r.at(-1), r.at(1)
        self.first = (send(0, own, 0, 1), send(1, own, 1, -1))
        self.second = (send(2, own, 1, 1), send(3, own, 0, -1))
        self.third = (send(4, left, 0, 1), send(5, right, 1, -1))

    def start(self):
        for c in self.first + self.second:
            c.start()

    def relay(self):
        for way in range(2):
            self.first[way].wait_recv()
            self.third[way].start()

    def wait(self):
        for c in self.second + self.third:
            c.wait_recv()

    def drain(self):
        for c in self.first + self.second + self.third:
            c.wait_send()


def kernel(peers, cap, tok, ids, codes, ograd, win_hbm, wout_hbm, out, tgrad, wing_hbm, woutg_hbm,
           win, wout, wing, woutg, s_tok, s_gr, r_tok, r_gr, s_eo, s_ig, r_eo, r_ig, x, g, chosen_at, w_hi, w_lo, acc,
           pre, hg, hid, unit,
           t_g, m_g, a_g, s_g, t2_g, m2_g, a2_g,
           t_u, m_u, a_u, s_u, t2_u, m2_u, a2_u,
           t_h, m_h, a_h, s_h, t2_h, m2_h, a2_h,
           t_k, m_k, a_k, s_k, t2_k, m2_k, a2_k,
           send_sems, recv_sems, a2a_send, a2a_recv, local):
    dp, me = lax.axis_index("dp"), lax.axis_index("expert")
    px, py = dp // SIDE, lax.rem(dp, SIDE)
    rows, ff = x.shape[0], wout.shape[0]
    grp, quarter = rows // SIDE, ff // SIDE
    hgrp = grp // 2
    slots = peers * ROW

    barrier = pltpu.get_barrier_semaphore()

    @pl.loop(1, peers)
    def _(r):
        pl.semaphore_signal(barrier, inc=1, device_id=(dp, lax.rem(me + r, peers)), device_id_type=MESH)

    for step in (1, SIDE - 1):
        pl.semaphore_signal(barrier, inc=1, device_id=(lax.rem(px + step, SIDE) * SIDE + py, me), device_id_type=MESH)
        pl.semaphore_signal(barrier, inc=1, device_id=(px * SIDE + lax.rem(py + step, SIDE), me), device_id_type=MESH)

    load_in = pltpu.make_async_copy(win_hbm, win, local.at[0])
    load_out = pltpu.make_async_copy(wout_hbm, wout, local.at[1])
    load_in.start()
    load_out.start()

    count = tok.shape[0]
    at_slot = lax.broadcasted_iota(jnp.int32, (count, slots), 1)
    expert_of = lax.rem(at_slot // ROW + me, peers)
    code_values = codes[...].astype(F32)
    shares = code_values / jnp.sum(code_values, axis=1, keepdims=True)
    names = ids[...]
    chosen = jnp.zeros((count, slots), F32)
    weight = jnp.zeros((count, slots), F32)
    for k in range(names.shape[1]):
        hit = names[:, k:k + 1] == expert_of
        chosen = jnp.where(hit, 1.0, chosen)
        weight = jnp.where(hit, shares[:, k:k + 1], weight)
    earlier = (lax.broadcasted_iota(jnp.int32, (count, count), 0)
               > lax.broadcasted_iota(jnp.int32, (count, count), 1)).astype(F32).astype(BF)
    rank = dot(earlier, chosen.astype(BF), 1, 0)
    place = lax.rem(at_slot, ROW).astype(F32)
    here = (chosen > 0.5) & (rank == place)
    placed = jnp.where(here, 1.0, 0.0).astype(BF)
    weight = jnp.where(here, weight, 0.0)
    high = weight.astype(BF)
    chosen_at[...] = placed
    w_hi[...] = high
    w_lo[...] = (weight - high.astype(F32)).astype(BF)
    s_tok[...] = dot(placed, tok[...], 0, 0).astype(BF).reshape(s_tok.shape)

    pl.semaphore_wait(barrier, peers - 1 + 4)

    def exchange(number, send, recv, sign):
        def go(r):
            pltpu.make_async_remote_copy(
                src_ref=send.at[r], dst_ref=recv.at[r], send_sem=a2a_send.at[number], recv_sem=a2a_recv.at[number],
                device_id=(dp, lax.rem(me + sign * r + peers, peers)), device_id_type=MESH).start()

        @pl.loop(1, peers // 2)
        def _(r):
            go(r)
            go(peers - r)

        go(peers // 2)
        recv[0] = send[0]
        whole = send.at[pl.ds(1, peers - 1)], recv.at[pl.ds(1, peers - 1)]
        return pltpu.make_async_remote_copy(
            src_ref=whole[0], dst_ref=whole[1], send_sem=a2a_send.at[number], recv_sem=a2a_recv.at[number],
            device_id=(dp, lax.rem(me + 1, peers)), device_id_type=MESH)

    to_x = exchange(0, s_tok, r_tok, 1)
    both = dot(w_hi[...], ograd[...], 0, 0) + dot(w_lo[...], ograd[...], 0, 0)
    s_gr[...] = both.astype(BF).reshape(s_gr.shape)
    to_g = exchange(1, s_gr, r_gr, 1)

    slot_row = lax.broadcasted_iota(jnp.int32, (rows, slots), 1)
    slot_pos = lax.rem(slot_row, ROW)
    packed_row = jnp.where(slot_pos < cap, slot_row // ROW * cap + slot_pos, -1)
    squeeze = (packed_row == lax.broadcasted_iota(jnp.int32, (rows, slots), 0)).astype(F32).astype(BF)

    x_dev = lambda q: (q * SIDE + py, me)
    y_dev = lambda q: (px * SIDE + q, me)
    used = [0]

    def ring(along_x):
        first = used[0]
        used[0] += 6
        return Ring(px if along_x else py, x_dev if along_x else y_dev,
                    send_sems.at[pl.ds(first, 6)], recv_sems.at[pl.ds(first, 6)])

    span = lambda q: pl.ds(pl.multiple_of(q * quarter, 128), quarter)

    def scatter_pair(src, row0, height, col0, x_first, bufs, split):
        tmp, mid, arr, s, tmp2, mid2, arr2 = bufs
        rows_at = pl.ds(row0, height)
        if x_first:
            half_width = 2 * quarter
            block = lambda q, h: src.at[q, rows_at, pl.ds(col0 + h * half_width, half_width)]
            whole = lambda q: src.at[q, rows_at, pl.ds(col0, 4 * quarter)]
            half = lambda ref, h: ref.at[:, pl.ds(h * half_width, half_width)]
            sub = lambda q: s.at[:, span(q)]
        else:
            cols = lambda q: pl.ds(pl.multiple_of(col0 + q * quarter, 128), quarter)
            block = lambda q, h: src.at[pl.ds(2 * h, 2), rows_at, cols(q)]
            whole = lambda q: src.at[:, rows_at, cols(q)]
            half = lambda ref, h: ref.at[pl.ds(2 * h, 2)]
            sub = lambda q: s.at[q]
        one = ReduceScatter(ring(x_first), block, tmp, mid, arr, half)
        cut = lambda h: pl.ds(0, split) if h == 0 else pl.ds(split, height - split)
        pick = lambda ref, h: ref.at[cut(h)]
        two = ReduceScatter2(ring(not x_first), lambda q, h: pick(sub(q), h), tmp2, mid2, arr2, pick)
        own = px if x_first else py
        other = py if x_first else px

        def join():
            one.wait()
            s[...] = (whole(own)[...].astype(F32) + arr[0].astype(F32) + arr[1].astype(F32)).astype(BF)

        def result():
            two.wait()
            return sub(other)[...].astype(F32) + arr2[0].astype(F32) + arr2[1].astype(F32)

        return one, join, two, result

    class ReduceScatter2(ReduceScatter):
        def __init__(self, ring_, block, tmp, summed, arrived, half):
            class Pair:
                def __init__(self, refs):
                    self.at = refs

                def __getitem__(self, i):
                    return self.at[i][...]

                def __setitem__(self, i, value):
                    self.at[i][...] = value

            super().__init__(ring_, block, Pair(tmp), Pair(summed), arrived, half)

    def gather_pair(dst, row0, height, col0, x_first_scatter, split):
        rows_at = pl.ds(row0, height)
        cut = lambda h: pl.ds(row0, split) if h == 0 else pl.ds(row0 + split, height - split)
        cols = lambda q: pl.ds(pl.multiple_of(col0 + q * quarter, 128), quarter)
        if x_first_scatter:
            one = AllGather(ring(False), lambda q, h: dst.at[px, cut(h), cols(q)])
            two = AllGather(ring(True), lambda q, h: dst.at[q, rows_at, pl.ds(col0 + 2 * h * quarter, 2 * quarter)])
        else:
            one = AllGather(ring(True), lambda q, h: dst.at[q, cut(h), cols(py)])
            two = AllGather(ring(False), lambda q, h: dst.at[pl.ds(2 * h, 2), rows_at, cols(q)])
        return one, two

    gate1, gate_join, gate2, gate_sum = scatter_pair(
        pre, 0, grp, 0, True, (t_g, m_g, a_g, s_g, t2_g, m2_g, a2_g), grp // 2)
    up1, up_join, up2, up_sum = scatter_pair(
        pre, 0, grp, ff, False, (t_u, m_u, a_u, s_u, t2_u, m2_u, a2_u), grp // 2)
    hga1, hga_join, hga2, hga_sum = scatter_pair(
        hg, 0, hgrp, 0, True, (t_h, m_h, a_h, s_h, t2_h, m2_h, a2_h), 32)
    hgb1, hgb_join, hgb2, hgb_sum = scatter_pair(
        hg, hgrp, hgrp, 0, False, (t_k, m_k, a_k, s_k, t2_k, m2_k, a2_k), 32)
    hida1, hida2 = gather_pair(hid, 0, hgrp, 0, True, 32)
    hidb1, hidb2 = gather_pair(hid, hgrp, hgrp, 0, False, 32)
    ug1, ug2 = gather_pair(unit, 0, grp, 0, True, grp // 2)
    uu1, uu2 = gather_pair(unit, 0, grp, ff, False, grp // 2)

    load_in.wait()
    to_x.wait_recv()
    x[...] = dot(squeeze, r_tok[...].reshape(slots, -1), 1, 0).astype(BF)

    @pl.loop(0, 2 * SIDE)
    def _(n):
        cols = span(n)
        pre[:, :, cols] = dot(x[...], win[:, cols], 1, 0).astype(BF).reshape(SIDE, grp, quarter)

    gate1.start()
    up1.start()
    gate1.relay()
    up1.relay()

    load_out.wait()
    to_g.wait_recv()
    g[...] = dot(squeeze, r_gr[...].reshape(slots, -1), 1, 0).astype(BF)

    @pl.loop(0, SIDE)
    def _(n):
        cols = span(n)
        hg[:, :, cols] = dot(g[...], wout[cols, :], 1, 1).astype(BF).reshape(SIDE, grp, quarter)

    gate_join()
    gate2.start()
    up_join()
    up2.start()
    hga1.start()
    hgb1.start()
    gate2.relay()
    up2.relay()
    hga1.relay()
    hgb1.relay()

    gate_pre, up_pre = gate_sum(), up_sum()
    active, slopes = activation(gate_pre)
    hidden = (active * up_pre).astype(BF)
    hid[px, :, span(py)] = hidden
    hida1.start()
    hidb1.start()

    hga_join()
    hga2.start()
    hgb_join()
    hgb2.start()
    hida1.relay()
    hidb1.relay()
    hga2.relay()
    hgb2.relay()
    hida1.wait()
    hida2.start()
    hidb1.wait()
    hidb2.start()

    hidden_grad = jnp.concatenate([hga_sum(), hgb_sum()], axis=0)
    unit[px, :, span(py)] = (hidden_grad * up_pre * slopes).astype(BF)
    unit[px, :, pl.ds(pl.multiple_of(ff + py * quarter, 128), quarter)] = (hidden_grad * active).astype(BF)
    ug1.start()
    uu1.start()
    hida2.relay()
    hidb2.relay()
    ug1.relay()
    uu1.relay()
    ug1.wait()
    ug2.start()
    uu1.wait()
    uu2.start()

    row_slot = lax.broadcasted_iota(jnp.int32, (slots, rows), 0)
    row_pos = lax.rem(row_slot, ROW)
    from_row = jnp.where(row_pos < cap, row_slot // ROW * cap + row_pos, -1)
    spread = (from_row == lax.broadcasted_iota(jnp.int32, (slots, rows), 1)).astype(F32).astype(BF)

    hida2.wait()
    hidb2.wait()
    acc[...] = jnp.zeros_like(acc)

    @pl.loop(0, SIDE)
    def _(n):
        cols = span(n)
        acc[...] += dot(hid[:, :, cols].reshape(rows, quarter), wout[cols, :], 1, 0)

    s_eo[...] = dot(spread, acc[...].astype(BF), 1, 0).astype(BF).reshape(s_eo.shape)
    from_eo = exchange(2, s_eo, r_eo, -1)

    ug2.relay()
    uu2.relay()

    @pl.loop(0, SIDE)
    def _(n):
        cols = span(n)
        woutg[cols, :] = dot(hid[:, :, cols].reshape(rows, quarter), g[...], 0, 0).astype(BF)

    store_out = pltpu.make_async_copy(woutg, woutg_hbm, local.at[2])
    store_out.start()

    ug2.wait()
    uu2.wait()
    acc[...] = jnp.zeros_like(acc)

    @pl.loop(0, 2 * SIDE)
    def _(n):
        cols = span(n)
        acc[...] += dot(unit[:, :, cols].reshape(rows, quarter), win[:, cols], 1, 1)

    s_ig[...] = dot(spread, acc[...].astype(BF), 1, 0).astype(BF).reshape(s_ig.shape)
    from_ig = exchange(3, s_ig, r_ig, -1)

    @pl.loop(0, 2 * SIDE)
    def _(n):
        cols = span(n)
        wing[:, cols] = dot(x[...], unit[:, :, cols].reshape(rows, quarter), 0, 0).astype(BF)

    store_in = pltpu.make_async_copy(wing, wing_hbm, local.at[3])
    store_in.start()

    from_eo.wait_recv()
    returned = r_eo[...].reshape(slots, -1)
    out[...] = (dot(w_hi[...], returned, 1, 0) + dot(w_lo[...], returned, 1, 0)).astype(BF)
    from_ig.wait_recv()
    tgrad[...] = dot(chosen_at[...], r_ig[...].reshape(slots, -1), 1, 0).astype(BF)

    for stage in (gate1, gate2, up1, up2, hga1, hga2, hgb1, hgb2, hida1, hida2, hidb1, hidb2, ug1, ug2, uu1, uu2):
        stage.drain()
    for moved in (to_x, to_g, from_eo, from_ig):
        moved.wait_send()
    store_out.wait()
    store_in.wait()


def body(tokens, expert_ids, gate_codes, out_grad, w_in, w_out):
    peers = lax.axis_size("expert")
    count, width = tokens.shape
    top = expert_ids.shape[1]
    ff = w_out.shape[1]
    cap = 3 * count * top // (2 * ALL_EXP)
    rows = cap * peers
    grp, quarter = rows // SIDE, ff // SIDE
    slots = peers * ROW
    vm = lambda *shape: pltpu.VMEM(shape, BF)

    def sums(height, x_first, split):
        if x_first:
            halves, block = (height, 2 * quarter), (height, 4 * quarter)
        else:
            halves, block = (2, height, quarter), (4, height, quarter)
        pair = [vm(split, quarter), vm(height - split, quarter)]
        return [vm(2, *halves), vm(2, *halves), vm(2, *block), vm(*block), pair, list(pair), vm(2, height, quarter)]

    message = vm(peers, ROW, width)
    scratch = [
        vm(width, 2 * ff), vm(ff, width), vm(width, 2 * ff), vm(ff, width),
        message, message, message, message, message, message, message, message,
        vm(rows, width), vm(rows, width), vm(count, slots), vm(count, slots), vm(count, slots),
        pltpu.VMEM((rows, width), F32),
        vm(SIDE, grp, 2 * ff), vm(SIDE, grp, ff), vm(SIDE, grp, ff), vm(SIDE, grp, 2 * ff),
        *sums(grp, True, grp // 2), *sums(grp, False, grp // 2),
        *sums(grp // 2, True, 32), *sums(grp // 2, False, 32),
        pltpu.SemaphoreType.DMA((96,)), pltpu.SemaphoreType.DMA((96,)),
        pltpu.SemaphoreType.DMA((4,)), pltpu.SemaphoreType.DMA((4,)), pltpu.SemaphoreType.DMA((4,)),
    ]
    vmem, hbm = pl.BlockSpec(memory_space=pltpu.VMEM), pl.BlockSpec(memory_space=pl.ANY)
    out, tgrad, wing, woutg = pl.pallas_call(
        functools.partial(kernel, peers, cap),
        out_shape=(
            jax.ShapeDtypeStruct((count, width), BF), jax.ShapeDtypeStruct((count, width), BF),
            jax.ShapeDtypeStruct((width, 2 * ff), BF), jax.ShapeDtypeStruct((ff, width), BF)),
        in_specs=[vmem, vmem, vmem, vmem, hbm, hbm],
        out_specs=(vmem, vmem, hbm, hbm),
        scratch_shapes=scratch,
        compiler_params=pltpu.CompilerParams(
            collective_id=0, has_side_effects=True, vmem_limit_bytes=56 * 1024 * 1024),
        cost_estimate=pl.CostEstimate(
            flops=2 * rows * width * ff * 9, bytes_accessed=12 * width * ff, transcendentals=grp * quarter),
    )(tokens, expert_ids, gate_codes, out_grad, w_in[0], w_out[0])
    return out, tgrad, wing[None], woutg[None]


def solution(mesh):
    placed = (
        P("expert", "dp"),
        P("expert", None),
        P("expert", None),
        P("expert", "dp"),
        P("expert", "dp", None),
        P("expert", None, "dp"),
    )
    return jax.shard_map(
        body,
        mesh=mesh,
        in_specs=placed,
        out_specs=(
            P("expert", "dp"),
            P("expert", "dp"),
            P("expert", "dp", None),
            P("expert", None, "dp"),
        ),
        check_vma=False,
    )
```

```python
import functools

import jax
import jax.numpy as jnp
from jax import lax
from jax.experimental import pallas as pl
from jax.experimental.pallas import tpu as pltpu
from jax.sharding import PartitionSpec as P

ALL_EXP = 128
SIDE = 4
LANES = 128
MESH = pl.DeviceIdType.MESH
BF = jnp.bfloat16
F32 = jnp.float32


def dot(a, b, ca, cb):
    return lax.dot_general(a, b, (((ca,), (cb,)), ((), ())), preferred_element_type=F32)


def activation(values):
    sigma = jax.nn.sigmoid(values)
    return values * sigma, sigma * (1.0 + values * (1.0 - sigma))


def iota(shape, axis):
    return lax.broadcasted_iota(jnp.int32, shape, axis)


def mask(condition):
    return jnp.where(condition, 1.0, 0.0).astype(BF)


class Move:
    def __init__(self, started, **kw):
        self.started, self.move = started, pltpu.make_async_remote_copy(device_id_type=MESH, **kw)
        self.arrived = self.left = False

    def start(self):
        self.move.start()
        self.started.append(self)

    def wait(self):
        self.arrived = True
        self.move.wait_recv()

    def leave(self):
        if not self.left:
            self.left = True
            self.move.wait_send()


class Ring:
    def __init__(self, started, place, device_of, send_sems, recv_sems):
        self.started, self.place, self.device_of = started, place, device_of
        self.send_sems, self.recv_sems = send_sems, recv_sems

    def at(self, step):
        return lax.rem(self.place + (step + SIDE), SIDE)

    def copy(self, number, src, dst, step):
        return Move(self.started, src_ref=src, dst_ref=dst, send_sem=self.send_sems.at[number],
                    recv_sem=self.recv_sems.at[number], device_id=self.device_of(self.at(step)))


class Stage:
    def start(self):
        for c in self.first + self.second:
            c.start()

    def wait(self):
        for c in self.second + self.third:
            c.wait()


class ReduceScatter(Stage):
    def __init__(self, ring, block, tmp, summed, arrived):
        self.ring, self.block, self.tmp, self.summed = ring, block, tmp, summed
        r = ring
        self.first = (r.copy(0, block(r.at(2), 0), tmp[0], 1), r.copy(1, block(r.at(2), 1), tmp[1], -1))
        self.second = (r.copy(2, block(r.at(1), 1), arrived(0, 1), 1), r.copy(3, block(r.at(-1), 0), arrived(1, 0), -1))
        self.third = (r.copy(4, summed[0], arrived(0, 0), 1), r.copy(5, summed[1], arrived(1, 1), -1))

    def relay(self):
        for way, (step, h) in enumerate(((1, 0), (-1, 1))):
            self.first[way].wait()
            mine = self.block(self.ring.at(step), h)[...]
            self.summed[way][...] = (mine.astype(F32) + self.tmp[way][...].astype(F32)).astype(BF)
            self.third[way].start()


class AllGather(Stage):
    def __init__(self, ring, region):
        r = ring
        send = lambda number, q, h, step: r.copy(number, region(q, h), region(q, h), step)
        own, left, right = r.at(0), r.at(-1), r.at(1)
        self.first = (send(0, own, 0, 1), send(1, own, 1, -1))
        self.second = (send(2, own, 1, 1), send(3, own, 0, -1))
        self.third = (send(4, left, 0, 1), send(5, right, 1, -1))

    def relay(self):
        for way in range(2):
            self.first[way].wait()
            self.third[way].start()


class Direct(Stage):
    def __init__(self, ring, out, into):
        self.moves = [ring.copy(way, out(ring.at(step)), into(way, ring.at(step)), step)
                      for way, step in enumerate((2, 1, -1))]

    def start(self):
        for c in self.moves:
            c.start()

    def wait(self):
        for c in self.moves:
            c.wait()


def span(q, width, first=0):
    return pl.ds(pl.multiple_of(q * width + first, LANES), width)


class Half:
    def __init__(self, x_first, height, width, src, dst, bufs, spots, ring):
        px, py = spots
        self.x_first, self.src, self.dst, self.width, self.spots = x_first, src, dst, width, spots
        tmp, mid, arr, s, arr2 = bufs
        self.arr, self.s, self.arr2 = arr, s, arr2
        wide = lambda h: pl.ds(h * 2 * width, 2 * width)
        pair = lambda h: pl.ds(2 * h, 2)
        if x_first:
            block = lambda q, h: src.at[q, :, wide(h)]
            self.whole = lambda: src.at[px]
            arrived = lambda way, h: arr.at[way, :, wide(h)]
            self.sub = lambda q: s.at[:, span(q, width)]
            own = dst.at[px, :, span(py, width)]
            region2 = lambda q, h: dst.at[q, :, wide(h)]
        else:
            block = lambda q, h: src.at[pair(h), :, span(q, width)]
            self.whole = lambda: src.at[:, :, span(py, width)]
            arrived = lambda way, h: arr.at[way, pair(h)]
            self.sub = lambda q: s.at[q]
            own = dst.at[px, :, span(py, width)]
            region2 = lambda q, h: dst.at[pair(h), :, span(q, width)]
        self.sum1 = ReduceScatter(ring(x_first), block, (tmp.at[0], tmp.at[1]), (mid.at[0], mid.at[1]), arrived)
        self.sum2 = Direct(ring(not x_first), self.sub, lambda way, q: arr2.at[way])
        self.get1 = Direct(ring(not x_first), lambda q: own, lambda way, q: own)
        self.get2 = AllGather(ring(x_first), region2)

    @staticmethod
    def scratch(x_first, height, width):
        vm = lambda *shape: pltpu.VMEM(shape, BF)
        half, block = ((height, 2 * width), (height, 4 * width)) if x_first else ((2, height, width), (4, height, width))
        return [vm(2, *half), vm(2, *half), vm(2, *block), vm(*block), vm(3, height, width)]

    def join(self):
        self.sum1.wait()
        self.s[...] = (self.whole()[...].astype(F32) + self.arr[0].astype(F32) + self.arr[1].astype(F32)).astype(BF)
        self.sum2.start()

    def result(self):
        self.sum2.wait()
        other = self.spots[1] if self.x_first else self.spots[0]
        return self.sub(other)[...].astype(F32) + sum(self.arr2[way].astype(F32) for way in range(3))

    def put(self, value):
        px, py = self.spots
        self.dst[px, :, span(py, self.width)] = value.astype(BF)
        self.get1.start()

    def onward(self):
        self.get1.wait()
        self.get2.start()


def both(halves, step, stage=None):
    for half in halves:
        getattr(getattr(half, stage) if stage else half, step)()


def steps(peers, cap, tok, ids, codes, ograd, win_hbm, wout_hbm, out, tgrad, wing_hbm, woutg_hbm,
          win, wout, wing, woutg, s1, s2, r1, r2, b1, b2, e1, e2, xs, gs, back1, back2,
          sq, sp, sq2, sp2, partial, gathered, bufs, send_sems, recv_sems, z_send, z_recv, local, started):
    dp, me = lax.axis_index("dp"), lax.axis_index("expert")
    px, py = dp // SIDE, lax.rem(dp, SIDE)
    ff, count = wout.shape[0], tok.shape[0]
    quarter = ff // SIDE
    height = partial[0].shape[1]
    rows = SIDE * height
    near = peers // 2
    edge = near // 2
    one, two = s1.shape[1], s2.shape[1]

    barrier = pltpu.get_barrier_semaphore()

    @pl.loop(1, peers)
    def _(r):
        pl.semaphore_signal(barrier, inc=1, device_id=(dp, lax.rem(me + r, peers)), device_id_type=MESH)

    for step in range(1, SIDE):
        pl.semaphore_signal(barrier, inc=1, device_id=(lax.rem(px + step, SIDE) * SIDE + py, me), device_id_type=MESH)
        pl.semaphore_signal(barrier, inc=1, device_id=(px * SIDE + lax.rem(py + step, SIDE), me), device_id_type=MESH)

    load_in = pltpu.make_async_copy(win_hbm, win, local.at[0])
    load_out = pltpu.make_async_copy(wout_hbm, wout, local.at[1])
    load_in.start()
    load_out.start()

    slot = iota((peers, count), 0)
    away = jnp.where(slot > edge, slot - edge, jnp.where(slot > 0, slot - edge - 1 + peers, 0))
    expert_of = lax.rem(away + me, peers)
    names = ids[...]
    code_values = codes[...].astype(F32)
    shares = code_values / jnp.sum(code_values, axis=0, keepdims=True)
    chosen = jnp.zeros((peers, count), F32)
    weight = jnp.zeros((peers, count), F32)
    for k in range(names.shape[0]):
        hit = names[k:k + 1, :] == expert_of
        chosen = jnp.where(hit, 1.0, chosen)
        weight = jnp.where(hit, shares[k:k + 1, :], weight)
    earlier = mask(iota((count, count), 0) < iota((count, count), 1))
    rank = dot(chosen.astype(BF), earlier, 1, 0)
    rank = jnp.where(chosen > 0.5, rank, 200.0).astype(BF)
    high = weight.astype(BF)
    low = (weight - high.astype(F32)).astype(BF)

    def places(size):
        widen = mask(iota((peers * size, peers), 0) // size == iota((peers * size, peers), 1))
        spot = lax.rem(iota((peers * size, count), 0), size)
        return spot, dot(widen, rank, 1, 0), dot(widen, high, 1, 0), dot(widen, low, 1, 0)

    keep = lambda here, value: jnp.where(here, value, 0.0).astype(BF)
    spot, at, hi, lo = places(one)
    left = (spot < cap) & (at == spot.astype(F32))
    right = (spot >= cap) & (spot < 2 * cap) & (at == (spot - cap).astype(F32))
    rest = (spot >= 2 * cap) & (at == (spot - 3 * cap + two).astype(F32))
    tokens, grads = tok[...], ograd[...]
    table = jnp.concatenate([mask(left), mask(right), keep(rest, hi), keep(rest, lo)], axis=1)
    values = jnp.concatenate([tokens[:, :LANES], tokens[:, LANES:], grads[:, LANES:], grads[:, LANES:]], axis=0)
    s1[...] = dot(table, values, 1, 0).astype(BF).reshape(s1.shape)
    back1[...] = table
    spot, at, hi, lo = places(two)
    left = (spot < cap) & (at == spot.astype(F32))
    right = (spot >= cap) & (at == (spot - cap).astype(F32))
    table = jnp.concatenate([keep(left, hi), keep(left, lo), keep(right, hi), keep(right, lo)], axis=1)
    values = jnp.concatenate([grads[:, :LANES], grads[:, :LANES], grads[:, LANES:], grads[:, LANES:]], axis=0)
    s2[...] = dot(table, values, 1, 0).astype(BF).reshape(s2.shape)
    back2[...] = table

    pl.semaphore_wait(barrier, peers - 1 + 2 * (SIDE - 1))

    def exchange(number, send, recv, chunk, sign):
        def go(k):
            away = jnp.where(k > edge, k - edge, k - edge - 1 + peers)
            pltpu.make_async_remote_copy(
                src_ref=send.at[k], dst_ref=recv.at[k], send_sem=z_send.at[number], recv_sem=z_recv.at[number],
                device_id=(dp, lax.rem(me + sign * away + peers, peers)), device_id_type=MESH).start()

        if chunk == 0:
            @pl.loop(0, edge - 1)
            def _(i):
                go(edge - i)
                go(edge + 1 + i)

            go(1)
            recv[0] = send[0]
        else:
            @pl.loop(0, near // 2)
            def _(i):
                go(near + i)
                go(peers - 1 - i)

        span_of = pl.ds(1, near - 1) if chunk == 0 else pl.ds(near, near)
        move = Move(started, src_ref=send.at[span_of], dst_ref=recv.at[span_of], send_sem=z_send.at[number],
                    recv_sem=z_recv.at[number], device_id=(dp, lax.rem(me + 1, peers)))
        started.append(move)
        return move

    x0 = exchange(0, s1, r1, 0, 1)
    g0 = exchange(1, s2, r2, 0, 1)
    x0.leave()
    g0.leave()
    x1 = exchange(2, s1, r1, 1, 1)
    g1 = exchange(3, s2, r2, 1, 1)
    def matches(size, shape, axis, first, last, shift):
        at, row = iota(shape, axis), iota(shape, 1 - axis)
        spot = lax.rem(at, size)
        return mask((spot >= first) & (spot < last) & (row == at // size * cap + spot - shift))

    for i, part in enumerate(((0, cap, 0), (cap, 2 * cap, cap), (2 * cap, one, 3 * cap - two))):
        sq[i] = matches(one, (rows, near * one), 1, *part)
        sp[i] = matches(one, (near * one, rows), 0, *part)
    for i, part in enumerate(((0, cap, 0), (cap, two, cap))):
        sq2[i] = matches(two, (rows, near * two), 1, *part)
        sp2[i] = matches(two, (near * two, rows), 0, *part)

    used = [0]

    def ring(along_x):
        first = used[0]
        used[0] += 6
        device_of = (lambda q: (q * SIDE + py, me)) if along_x else (lambda q: (px * SIDE + q, me))
        return Ring(started, px if along_x else py, device_of, send_sems.at[pl.ds(first, 6)], recv_sems.at[pl.ds(first, 6)])

    halves = [Half(i % 2 == 0, height, partial[i].shape[2] // SIDE, partial[i], gathered[i], bufs[i], (px, py), ring)
              for i in range(6)]
    a, pre, hg = halves[0:2], halves[2:4], halves[4:6]

    def take_x(chunk):
        got = r1[pl.ds(chunk * near, near)].reshape(near * one, LANES)
        xs[chunk] = jnp.concatenate([dot(sq[0], got, 1, 0), dot(sq[1], got, 1, 0)], axis=1).astype(BF)

    def take_g(chunk):
        got = r1[pl.ds(chunk * near, near)].reshape(near * one, LANES)
        got2 = r2[pl.ds(chunk * near, near)].reshape(near * two, LANES)
        gs[chunk] = jnp.concatenate(
            [dot(sq2[0], got2, 1, 0), dot(sq2[1], got2, 1, 0) + dot(sq[2], got, 1, 0)], axis=1).astype(BF)

    def products(chunk, ref, first, width, left, q):
        ref[:, :, pl.ds(pl.multiple_of(q * (ref.shape[2] // SIDE) + first, LANES), width)] = (
            left.astype(BF).reshape(SIDE, height, width))

    cut0, cut1 = 256, 128

    load_in.wait()
    load_out.wait()
    x0.wait()
    g0.wait()
    take_x(0)
    take_g(0)

    @pl.loop(0, SIDE)
    def _(q):
        products(0, partial[0], 0, quarter, dot(xs[0], win[:, span(q, quarter)], 1, 0), q)
        products(0, partial[1], 0, quarter, dot(xs[0], win[:, span(q, quarter, ff)], 1, 0), q)
        grad = dot(gs[0], wout[span(q, quarter), :], 1, 1)
        products(0, partial[0], quarter, cut0, grad[:, :cut0], q)
        products(0, partial[1], quarter, quarter - cut0, grad[:, cut0:], q)

    both(a, "start", "sum1")
    both(a, "relay", "sum1")
    both(a, "join")

    x1.wait()
    take_x(1)

    @pl.loop(0, SIDE)
    def _(q):
        products(1, partial[2], 0, quarter, dot(xs[1], win[:, span(q, quarter)], 1, 0), q)
        products(1, partial[3], 0, quarter, dot(xs[1], win[:, span(q, quarter, ff)], 1, 0), q)

    both(pre, "start", "sum1")

    first, second = a[0].result(), a[1].result()
    gate_pre, up_pre = first[:, :quarter], second[:, :quarter]
    hidden_grad = jnp.concatenate([first[:, quarter:], second[:, quarter:]], axis=1)
    active, slopes = activation(gate_pre)
    hidden = active * up_pre
    a[0].put(jnp.concatenate([hidden_grad * up_pre * slopes, hidden[:, :cut0]], axis=1))
    a[1].put(jnp.concatenate([hidden_grad * active, hidden[:, cut0:]], axis=1))

    both(pre, "relay", "sum1")

    g1.wait()
    take_g(1)

    @pl.loop(0, SIDE)
    def _(q):
        grad = dot(gs[1], wout[span(q, quarter), :], 1, 1)
        products(1, partial[4], 0, cut1, grad[:, :cut1], q)
        products(1, partial[5], 0, quarter - cut1, grad[:, cut1:], q)

    both(hg, "start", "sum1")
    both(pre, "join")
    both(hg, "relay", "sum1")
    both(a, "onward")
    both(hg, "join")

    gate_pre, up_pre = pre[0].result(), pre[1].result()
    active, slopes = activation(gate_pre)
    hidden = active * up_pre
    hg[0].put(hidden[:, :cut1])
    hg[1].put(hidden[:, cut1:])
    hidden_grad = jnp.concatenate([hg[0].result(), hg[1].result()], axis=1)
    pre[0].put(hidden_grad * up_pre * slopes)
    pre[1].put(hidden_grad * active)
    both(a, "relay", "get2")
    both(hg, "onward")
    both(pre, "onward")
    both(hg, "relay", "get2")

    flat = lambda ref, where: ref[:, :, where].reshape(rows, -1)
    at = lambda q, chunk, first, width: pl.ds(pl.multiple_of(q * (gathered[chunk].shape[2] // SIDE) + first, LANES), width)

    def hidden_of(chunk, q):
        i, first, cut = (0, quarter, cut0) if chunk == 0 else (4, 0, cut1)
        return (flat(gathered[i], at(q, i, first, cut)), flat(gathered[i + 1], at(q, i + 1, first, quarter - cut)), cut)

    def unit_of(chunk, part, q):
        i = part if chunk == 0 else 2 + part
        return flat(gathered[i], at(q, i, 0, quarter))

    def outs(chunk):
        total = jnp.zeros((rows, 2 * LANES), F32)
        for q in range(SIDE):
            left, right, cut = hidden_of(chunk, q)
            total += dot(left, wout[pl.ds(q * quarter, cut), :], 1, 0)
            total += dot(right, wout[pl.ds(q * quarter + cut, quarter - cut), :], 1, 0)
        return total.astype(BF)

    def inputs(chunk):
        total = jnp.zeros((rows, 2 * LANES), F32)
        for part in range(2):
            for q in range(SIDE):
                total += dot(unit_of(chunk, part, q), win[:, pl.ds(part * ff + q * quarter, quarter)], 1, 1)
        return total.astype(BF)

    def return_outs(chunk, outs_):
        left, right = outs_[:, :LANES], outs_[:, LANES:]
        b2[pl.ds(chunk * near, near)] = (dot(sp2[0], left, 1, 0) + dot(sp2[1], right, 1, 0)).astype(BF).reshape(near, two, LANES)
        return exchange(4 + chunk, b2, e2, chunk, -1)

    def return_inputs(chunk, outs_, inputs_):
        left, right = inputs_[:, :LANES], inputs_[:, LANES:]
        b1[pl.ds(chunk * near, near)] = (
            dot(sp[0], left, 1, 0) + dot(sp[1], right, 1, 0) + dot(sp[2], outs_[:, LANES:], 1, 0)
        ).astype(BF).reshape(near, one, LANES)
        return exchange(6 + chunk, b1, e1, chunk, -1)

    both(a, "wait", "get2")
    near_outs = outs(0)
    eo0 = return_outs(0, near_outs)
    ig0 = return_inputs(0, near_outs, inputs(0))
    both(pre, "relay", "get2")
    both(hg, "wait", "get2")
    far_outs = outs(1)
    eo1 = return_outs(1, far_outs)

    @pl.loop(0, SIDE)
    def _(q):
        left0, right0, _ = hidden_of(0, q)
        left1, right1, _ = hidden_of(1, q)
        hidden0 = jnp.concatenate([left0, right0], axis=1)
        hidden1 = jnp.concatenate([left1, right1], axis=1)
        woutg[span(q, quarter), :] = (dot(hidden0, gs[0], 0, 0) + dot(hidden1, gs[1], 0, 0)).astype(BF)

    store_out = pltpu.make_async_copy(woutg, woutg_hbm, local.at[2])
    store_out.start()

    both(pre, "wait", "get2")
    ig1 = return_inputs(1, far_outs, inputs(1))

    for part in range(2):
        @pl.loop(0, SIDE)
        def _(q):
            wing[:, span(q, quarter, part * ff)] = (
                dot(xs[0], unit_of(0, part, q), 0, 0) + dot(xs[1], unit_of(1, part, q), 0, 0)).astype(BF)

    store_in = pltpu.make_async_copy(wing, wing_hbm, local.at[3])
    store_in.start()

    eo0.wait()
    eo1.wait()
    ret2 = e2[...].reshape(peers * two, LANES)
    sides = [dot(back2[:, pl.ds(i * LANES, LANES)], ret2, 0, 0) for i in range(4)]
    ig0.wait()
    ig1.wait()
    ret1 = e1[...].reshape(peers * one, LANES)
    ends = [dot(back1[:, pl.ds(i * LANES, LANES)], ret1, 0, 0) for i in range(4)]
    out[...] = jnp.concatenate([sides[0] + sides[1], sides[2] + sides[3] + ends[2] + ends[3]], axis=1).astype(BF)
    tgrad[...] = jnp.concatenate([ends[0], ends[1]], axis=1).astype(BF)
    store_out.wait()
    store_in.wait()


def kernel(peers, cap, *refs):
    started = []
    steps(peers, cap, *refs, started)
    for move in started:
        if not move.arrived:
            move.wait()
    for move in started:
        move.leave()


def finish(parts, *refs):
    srcs, dsts, holds, ins, outs = refs[:4], refs[4:8], refs[8:12], refs[12], refs[13]
    ways = []
    for src, dst, hold, cuts in zip(srcs, dsts, holds, parts):
        step = src.shape[0] // cuts
        for i in range(cuts):
            at, n = pl.ds(i * step, step), len(ways)
            ways.append((pltpu.make_async_copy(src.at[at], hold.at[at], ins.at[n]),
                         pltpu.make_async_copy(hold.at[at], dst.at[at], outs.at[n])))
    for load, _ in ways:
        load.start()
    for load, store in ways:
        load.wait()
        store.start()
    for _, store in ways:
        store.wait()


def body(tokens, expert_ids, gate_codes, out_grad, w_in, w_out):
    peers = lax.axis_size("expert")
    count, width = tokens.shape
    top = expert_ids.shape[1]
    ff = w_out.shape[1]
    cap = 3 * count * top // (2 * ALL_EXP)
    rows = cap * peers // 2
    height, quarter = rows // SIDE, ff // SIDE
    one, two = 32, 16
    vm = lambda *shape: pltpu.VMEM(shape, BF)
    widths = (quarter + 256, quarter + 128, quarter, quarter, 128, 256)
    m1, m2 = vm(peers, one, LANES), vm(peers, two, LANES)
    scratch = [
        vm(width, 2 * ff), vm(ff, width), vm(width, 2 * ff), vm(ff, width),
        m1, m2, m1, m2, m1, m2, m1, m2,
        vm(2, rows, width), vm(2, rows, width),
        vm(peers * one, 4 * count), vm(peers * two, 4 * count),
        vm(3, rows, peers // 2 * one), vm(3, peers // 2 * one, rows),
        vm(2, rows, peers // 2 * two), vm(2, peers // 2 * two, rows),
        [vm(SIDE, height, SIDE * w) for w in widths],
        [vm(SIDE, height, SIDE * w) for w in widths],
        [Half.scratch(i % 2 == 0, height, w) for i, w in enumerate(widths)],
        pltpu.SemaphoreType.DMA((144,)), pltpu.SemaphoreType.DMA((144,)),
        pltpu.SemaphoreType.DMA((8,)), pltpu.SemaphoreType.DMA((8,)), pltpu.SemaphoreType.DMA((4,)),
    ]
    vmem, hbm = pl.BlockSpec(memory_space=pltpu.VMEM), pl.BlockSpec(memory_space=pl.ANY)
    shapes = (
        jax.ShapeDtypeStruct((count, width), BF), jax.ShapeDtypeStruct((count, width), BF),
        jax.ShapeDtypeStruct((width, 2 * ff), BF), jax.ShapeDtypeStruct((ff, width), BF))
    results = pl.pallas_call(
        functools.partial(kernel, peers, cap),
        out_shape=shapes,
        in_specs=[vmem, vmem, vmem, vmem, hbm, hbm],
        out_specs=(vmem, vmem, hbm, hbm),
        scratch_shapes=scratch,
        compiler_params=pltpu.CompilerParams(
            collective_id=0, has_side_effects=True, vmem_limit_bytes=56 * 1024 * 1024),
        cost_estimate=pl.CostEstimate(
            flops=4 * rows * width * ff * 9, bytes_accessed=12 * width * ff, transcendentals=rows * quarter),
    )(tokens, expert_ids.T, gate_codes.T, out_grad, w_in[0], w_out[0])
    out, tgrad, wing, woutg = pl.pallas_call(
        functools.partial(finish, (1, 1, 4, 2)),
        out_shape=shapes,
        in_specs=[hbm] * 4,
        out_specs=(hbm,) * 4,
        scratch_shapes=[pltpu.VMEM(s.shape, BF) for s in shapes] + [pltpu.SemaphoreType.DMA((8,))] * 2,
    )(*results)
    return out, tgrad, wing[None], woutg[None]


def solution(mesh):
    placed = (
        P("expert", "dp"),
        P("expert", None),
        P("expert", None),
        P("expert", "dp"),
        P("expert", "dp", None),
        P("expert", None, "dp"),
    )
    return jax.shard_map(
        body,
        mesh=mesh,
        in_specs=placed,
        out_specs=(
            P("expert", "dp"),
            P("expert", "dp"),
            P("expert", "dp", None),
            P("expert", None, "dp"),
        ),
        check_vma=False,
    )
```

```python
import functools

import jax
import jax.numpy as jnp
from jax import lax
from jax.experimental import pallas as pl
from jax.experimental.pallas import tpu as pltpu
from jax.sharding import PartitionSpec as P

ALL_EXP = 128
SIDE = 4
LANES = 128
MESH = pl.DeviceIdType.MESH
BF = jnp.bfloat16
F32 = jnp.float32


def dot(a, b, ca, cb):
    return lax.dot_general(a, b, (((ca,), (cb,)), ((), ())), preferred_element_type=F32)


def activation(values):
    sigma = jax.nn.sigmoid(values)
    return values * sigma, sigma * (1.0 + values * (1.0 - sigma))


def iota(shape, axis):
    return lax.broadcasted_iota(jnp.int32, shape, axis)


def mask(condition):
    return jnp.where(condition, 1.0, 0.0).astype(BF)


class Move:
    def __init__(self, started, **kw):
        self.started, self.move = started, pltpu.make_async_remote_copy(device_id_type=MESH, **kw)
        self.arrived = self.left = False

    def start(self):
        self.move.start()
        self.started.append(self)

    def wait(self):
        self.arrived = True
        self.move.wait_recv()

    def leave(self):
        if not self.left:
            self.left = True
            self.move.wait_send()


class Ring:
    def __init__(self, started, place, device_of, send_sems, recv_sems):
        self.started, self.place, self.device_of = started, place, device_of
        self.send_sems, self.recv_sems = send_sems, recv_sems

    def at(self, step):
        return lax.rem(self.place + (step + SIDE), SIDE)

    def copy(self, number, src, dst, step):
        return Move(self.started, src_ref=src, dst_ref=dst, send_sem=self.send_sems.at[number],
                    recv_sem=self.recv_sems.at[number], device_id=self.device_of(self.at(step)))


class Stage:
    def start(self):
        for c in self.first + self.second:
            c.start()

    def wait(self):
        for c in self.second + self.third:
            c.wait()


class ReduceScatter(Stage):
    def __init__(self, ring, block, tmp, summed, arrived):
        self.ring, self.block, self.tmp, self.summed = ring, block, tmp, summed
        r = ring
        self.first = (r.copy(0, block(r.at(2), 0), tmp[0], 1), r.copy(1, block(r.at(2), 1), tmp[1], -1))
        self.second = (r.copy(2, block(r.at(1), 1), arrived(0, 1), 1), r.copy(3, block(r.at(-1), 0), arrived(1, 0), -1))
        self.third = (r.copy(4, summed[0], arrived(0, 0), 1), r.copy(5, summed[1], arrived(1, 1), -1))

    def relay(self):
        for way, (step, h) in enumerate(((1, 0), (-1, 1))):
            self.first[way].wait()
            mine = self.block(self.ring.at(step), h)[...]
            self.summed[way][...] = (mine.astype(F32) + self.tmp[way][...].astype(F32)).astype(BF)
            self.third[way].start()


class AllGather(Stage):
    def __init__(self, ring, region):
        r = ring
        send = lambda number, q, h, step: r.copy(number, region(q, h), region(q, h), step)
        own, left, right = r.at(0), r.at(-1), r.at(1)
        self.first = (send(0, own, 0, 1), send(1, own, 1, -1))
        self.second = (send(2, own, 1, 1), send(3, own, 0, -1))
        self.third = (send(4, left, 0, 1), send(5, right, 1, -1))

    def relay(self):
        for way in range(2):
            self.first[way].wait()
            self.third[way].start()


class Direct(Stage):
    def __init__(self, ring, out, into):
        self.moves = [ring.copy(way, out(ring.at(step)), into(way, ring.at(step)), step)
                      for way, step in enumerate((2, 1, -1))]

    def start(self):
        for c in self.moves:
            c.start()

    def wait(self):
        for c in self.moves:
            c.wait()


def span(q, width, first=0):
    return pl.ds(pl.multiple_of(q * width + first, LANES), width)


class Half:
    def __init__(self, x_first, height, width, src, dst, bufs, spots, ring):
        px, py = spots
        self.x_first, self.src, self.dst, self.width, self.spots = x_first, src, dst, width, spots
        tmp, mid, arr, s, arr2 = bufs
        self.arr, self.s, self.arr2 = arr, s, arr2
        wide = lambda h: pl.ds(h * 2 * width, 2 * width)
        pair = lambda h: pl.ds(2 * h, 2)
        if x_first:
            block = lambda q, h: src.at[q, :, wide(h)]
            self.whole = lambda: src.at[px]
            arrived = lambda way, h: arr.at[way, :, wide(h)]
            self.sub = lambda q: s.at[:, span(q, width)]
            own = dst.at[px, :, span(py, width)]
            region2 = lambda q, h: dst.at[q, :, wide(h)]
        else:
            block = lambda q, h: src.at[pair(h), :, span(q, width)]
            self.whole = lambda: src.at[:, :, span(py, width)]
            arrived = lambda way, h: arr.at[way, pair(h)]
            self.sub = lambda q: s.at[q]
            own = dst.at[px, :, span(py, width)]
            region2 = lambda q, h: dst.at[pair(h), :, span(q, width)]
        self.sum1 = ReduceScatter(ring(x_first), block, (tmp.at[0], tmp.at[1]), (mid.at[0], mid.at[1]), arrived)
        self.sum2 = Direct(ring(not x_first), self.sub, lambda way, q: arr2.at[way])
        self.get1 = Direct(ring(not x_first), lambda q: own, lambda way, q: own)
        self.get2 = AllGather(ring(x_first), region2)

    @staticmethod
    def scratch(x_first, height, width):
        vm = lambda *shape: pltpu.VMEM(shape, BF)
        half, block = ((height, 2 * width), (height, 4 * width)) if x_first else ((2, height, width), (4, height, width))
        return [vm(2, *half), vm(2, *half), vm(2, *block), vm(*block), vm(3, height, width)]

    def join(self):
        self.sum1.wait()
        self.s[...] = (self.whole()[...].astype(F32) + self.arr[0].astype(F32) + self.arr[1].astype(F32)).astype(BF)
        self.sum2.start()

    def result(self):
        self.sum2.wait()
        other = self.spots[1] if self.x_first else self.spots[0]
        return self.sub(other)[...].astype(F32) + sum(self.arr2[way].astype(F32) for way in range(3))

    def put(self, value):
        px, py = self.spots
        self.dst[px, :, span(py, self.width)] = value.astype(BF)
        self.get1.start()

    def onward(self):
        self.get1.wait()
        self.get2.start()


def both(halves, step, stage=None):
    for half in halves:
        getattr(getattr(half, stage) if stage else half, step)()


def steps(peers, cap, tok, ids, codes, ograd, win_hbm, wout_hbm, out, tgrad, wing_hbm, woutg_hbm,
          win, wout, wing, woutg, s1, s2, r1, r2, b1, b2, e1, e2, xs, gs, back1, back2,
          sq, sp, sq2, sp2, partial, gathered, bufs, send_sems, recv_sems, z_send, z_recv, local, started):
    dp, me = lax.axis_index("dp"), lax.axis_index("expert")
    px, py = dp // SIDE, lax.rem(dp, SIDE)
    ff, count = wout.shape[0], tok.shape[0]
    quarter = ff // SIDE
    height = partial[0].shape[1]
    rows = SIDE * height
    near = peers // 2
    edge = near // 2
    one, two = s1.shape[1], s2.shape[1]

    barrier = pltpu.get_barrier_semaphore()

    @pl.loop(1, peers)
    def _(r):
        pl.semaphore_signal(barrier, inc=1, device_id=(dp, lax.rem(me + r, peers)), device_id_type=MESH)

    for step in range(1, SIDE):
        pl.semaphore_signal(barrier, inc=1, device_id=(lax.rem(px + step, SIDE) * SIDE + py, me), device_id_type=MESH)
        pl.semaphore_signal(barrier, inc=1, device_id=(px * SIDE + lax.rem(py + step, SIDE), me), device_id_type=MESH)

    load_in = pltpu.make_async_copy(win_hbm, win, local.at[0])
    load_out = pltpu.make_async_copy(wout_hbm, wout, local.at[1])
    load_in.start()
    load_out.start()

    slot = iota((peers, count), 0)
    away = jnp.where(slot > edge, slot - edge, jnp.where(slot > 0, slot - edge - 1 + peers, 0))
    expert_of = lax.rem(away + me, peers)
    names = ids[...]
    code_values = codes[...].astype(F32)
    shares = code_values / jnp.sum(code_values, axis=0, keepdims=True)
    chosen = jnp.zeros((peers, count), F32)
    weight = jnp.zeros((peers, count), F32)
    for k in range(names.shape[0]):
        hit = names[k:k + 1, :] == expert_of
        chosen = jnp.where(hit, 1.0, chosen)
        weight = jnp.where(hit, shares[k:k + 1, :], weight)
    earlier = mask(iota((count, count), 0) < iota((count, count), 1))
    rank = dot(chosen.astype(BF), earlier, 1, 0)
    rank = jnp.where(chosen > 0.5, rank, 200.0).astype(BF)
    high = weight.astype(BF)
    low = (weight - high.astype(F32)).astype(BF)

    def places(size):
        widen = mask(iota((peers * size, peers), 0) // size == iota((peers * size, peers), 1))
        spot = lax.rem(iota((peers * size, count), 0), size)
        return spot, dot(widen, rank, 1, 0), dot(widen, high, 1, 0), dot(widen, low, 1, 0)

    keep = lambda here, value: jnp.where(here, value, 0.0).astype(BF)
    spot, at, hi, lo = places(one)
    left = (spot < cap) & (at == spot.astype(F32))
    right = (spot >= cap) & (spot < 2 * cap) & (at == (spot - cap).astype(F32))
    rest = (spot >= 2 * cap) & (at == (spot - 3 * cap + two).astype(F32))
    tokens, grads = tok[...], ograd[...]
    table = jnp.concatenate([mask(left), mask(right), keep(rest, hi), keep(rest, lo)], axis=1)
    values = jnp.concatenate([tokens[:, :LANES], tokens[:, LANES:], grads[:, LANES:], grads[:, LANES:]], axis=0)
    s1[...] = dot(table, values, 1, 0).astype(BF).reshape(s1.shape)
    back1[...] = table
    spot, at, hi, lo = places(two)
    left = (spot < cap) & (at == spot.astype(F32))
    right = (spot >= cap) & (at == (spot - cap).astype(F32))
    table = jnp.concatenate([keep(left, hi), keep(left, lo), keep(right, hi), keep(right, lo)], axis=1)
    values = jnp.concatenate([grads[:, :LANES], grads[:, :LANES], grads[:, LANES:], grads[:, LANES:]], axis=0)
    s2[...] = dot(table, values, 1, 0).astype(BF).reshape(s2.shape)
    back2[...] = table

    pl.semaphore_wait(barrier, peers - 1 + 2 * (SIDE - 1))

    def exchange(number, send, recv, chunk, sign):
        def go(k):
            away = jnp.where(k > edge, k - edge, k - edge - 1 + peers)
            pltpu.make_async_remote_copy(
                src_ref=send.at[k], dst_ref=recv.at[k], send_sem=z_send.at[number], recv_sem=z_recv.at[number],
                device_id=(dp, lax.rem(me + sign * away + peers, peers)), device_id_type=MESH).start()

        if chunk == 0:
            @pl.loop(0, edge - 1)
            def _(i):
                go(edge - i)
                go(edge + 1 + i)

            go(1)
            recv[0] = send[0]
        else:
            @pl.loop(0, near // 2)
            def _(i):
                go(near + i)
                go(peers - 1 - i)

        span_of = pl.ds(1, near - 1) if chunk == 0 else pl.ds(near, near)
        move = Move(started, src_ref=send.at[span_of], dst_ref=recv.at[span_of], send_sem=z_send.at[number],
                    recv_sem=z_recv.at[number], device_id=(dp, lax.rem(me + 1, peers)))
        started.append(move)
        return move

    x0 = exchange(0, s1, r1, 0, 1)
    g0 = exchange(1, s2, r2, 0, 1)
    x0.leave()
    g0.leave()
    x1 = exchange(2, s1, r1, 1, 1)
    g1 = exchange(3, s2, r2, 1, 1)
    def matches(size, shape, axis, first, last, shift):
        at, row = iota(shape, axis), iota(shape, 1 - axis)
        spot = lax.rem(at, size)
        return mask((spot >= first) & (spot < last) & (row == at // size * cap + spot - shift))

    for i, part in enumerate(((0, cap, 0), (cap, 2 * cap, cap), (2 * cap, one, 3 * cap - two))):
        sq[i] = matches(one, (rows, near * one), 1, *part)
        sp[i] = matches(one, (near * one, rows), 0, *part)
    for i, part in enumerate(((0, cap, 0), (cap, two, cap))):
        sq2[i] = matches(two, (rows, near * two), 1, *part)
        sp2[i] = matches(two, (near * two, rows), 0, *part)

    used = [0]

    def ring(along_x):
        first = used[0]
        used[0] += 6
        device_of = (lambda q: (q * SIDE + py, me)) if along_x else (lambda q: (px * SIDE + q, me))
        return Ring(started, px if along_x else py, device_of, send_sems.at[pl.ds(first, 6)], recv_sems.at[pl.ds(first, 6)])

    halves = [Half(i % 2 == 0, height, partial[i].shape[2] // SIDE, partial[i], gathered[i], bufs[i], (px, py), ring)
              for i in range(6)]
    a, pre, hg = halves[0:2], halves[2:4], halves[4:6]

    def take_x(chunk):
        got = r1[pl.ds(chunk * near, near)].reshape(near * one, LANES)
        xs[chunk] = jnp.concatenate([dot(sq[0], got, 1, 0), dot(sq[1], got, 1, 0)], axis=1).astype(BF)

    def take_g(chunk):
        got = r1[pl.ds(chunk * near, near)].reshape(near * one, LANES)
        got2 = r2[pl.ds(chunk * near, near)].reshape(near * two, LANES)
        gs[chunk] = jnp.concatenate(
            [dot(sq2[0], got2, 1, 0), dot(sq2[1], got2, 1, 0) + dot(sq[2], got, 1, 0)], axis=1).astype(BF)

    def products(chunk, ref, first, width, left, q):
        ref[:, :, pl.ds(pl.multiple_of(q * (ref.shape[2] // SIDE) + first, LANES), width)] = (
            left.astype(BF).reshape(SIDE, height, width))

    cut0, cut1 = 256, 128

    load_in.wait()
    load_out.wait()
    x0.wait()
    g0.wait()
    take_x(0)
    take_g(0)

    @pl.loop(0, SIDE)
    def _(q):
        products(0, partial[0], 0, quarter, dot(xs[0], win[:, span(q, quarter)], 1, 0), q)
        products(0, partial[1], 0, quarter, dot(xs[0], win[:, span(q, quarter, ff)], 1, 0), q)
        grad = dot(gs[0], wout[span(q, quarter), :], 1, 1)
        products(0, partial[0], quarter, cut0, grad[:, :cut0], q)
        products(0, partial[1], quarter, quarter - cut0, grad[:, cut0:], q)

    both(a, "start", "sum1")
    both(a, "relay", "sum1")
    both(a, "join")

    x1.wait()
    take_x(1)

    @pl.loop(0, SIDE)
    def _(q):
        products(1, partial[2], 0, quarter, dot(xs[1], win[:, span(q, quarter)], 1, 0), q)
        products(1, partial[3], 0, quarter, dot(xs[1], win[:, span(q, quarter, ff)], 1, 0), q)

    both(pre, "start", "sum1")

    first, second = a[0].result(), a[1].result()
    gate_pre, up_pre = first[:, :quarter], second[:, :quarter]
    hidden_grad = jnp.concatenate([first[:, quarter:], second[:, quarter:]], axis=1)
    active, slopes = activation(gate_pre)
    hidden = active * up_pre
    a[0].put(jnp.concatenate([hidden_grad * up_pre * slopes, hidden[:, :cut0]], axis=1))
    a[1].put(jnp.concatenate([hidden_grad * active, hidden[:, cut0:]], axis=1))

    both(pre, "relay", "sum1")

    g1.wait()
    take_g(1)

    @pl.loop(0, SIDE)
    def _(q):
        grad = dot(gs[1], wout[span(q, quarter), :], 1, 1)
        products(1, partial[4], 0, cut1, grad[:, :cut1], q)
        products(1, partial[5], 0, quarter - cut1, grad[:, cut1:], q)

    both(hg, "start", "sum1")
    both(pre, "join")
    both(hg, "relay", "sum1")
    both(a, "onward")
    both(hg, "join")

    gate_pre, up_pre = pre[0].result(), pre[1].result()
    active, slopes = activation(gate_pre)
    hidden = active * up_pre
    hg[0].put(hidden[:, :cut1])
    hg[1].put(hidden[:, cut1:])
    both(a, "relay", "get2")
    hidden_grad = jnp.concatenate([hg[0].result(), hg[1].result()], axis=1)
    pre[0].put(hidden_grad * up_pre * slopes)
    pre[1].put(hidden_grad * active)
    both(hg, "onward")
    both(pre, "onward")
    flat = lambda ref, where: ref[:, :, where].reshape(rows, -1)
    at = lambda q, chunk, first, width: pl.ds(pl.multiple_of(q * (gathered[chunk].shape[2] // SIDE) + first, LANES), width)

    def hidden_of(chunk, q):
        i, first, cut = (0, quarter, cut0) if chunk == 0 else (4, 0, cut1)
        return (flat(gathered[i], at(q, i, first, cut)), flat(gathered[i + 1], at(q, i + 1, first, quarter - cut)), cut)

    def unit_of(chunk, part, q):
        i = part if chunk == 0 else 2 + part
        return flat(gathered[i], at(q, i, 0, quarter))

    def outs(chunk):
        total = jnp.zeros((rows, 2 * LANES), F32)
        for q in range(SIDE):
            left, right, cut = hidden_of(chunk, q)
            total += dot(left, wout[pl.ds(q * quarter, cut), :], 1, 0)
            total += dot(right, wout[pl.ds(q * quarter + cut, quarter - cut), :], 1, 0)
        return total.astype(BF)

    def inputs(chunk):
        total = jnp.zeros((rows, 2 * LANES), F32)
        for part in range(2):
            for q in range(SIDE):
                total += dot(unit_of(chunk, part, q), win[:, pl.ds(part * ff + q * quarter, quarter)], 1, 1)
        return total.astype(BF)

    def return_outs(chunk, outs_):
        left, right = outs_[:, :LANES], outs_[:, LANES:]
        b2[pl.ds(chunk * near, near)] = (dot(sp2[0], left, 1, 0) + dot(sp2[1], right, 1, 0)).astype(BF).reshape(near, two, LANES)
        return exchange(4 + chunk, b2, e2, chunk, -1)

    def return_inputs(chunk, outs_, inputs_):
        left, right = inputs_[:, :LANES], inputs_[:, LANES:]
        b1[pl.ds(chunk * near, near)] = (
            dot(sp[0], left, 1, 0) + dot(sp[1], right, 1, 0) + dot(sp[2], outs_[:, LANES:], 1, 0)
        ).astype(BF).reshape(near, one, LANES)
        return exchange(6 + chunk, b1, e1, chunk, -1)

    both(a, "wait", "get2")
    near_outs = outs(0)
    eo0 = return_outs(0, near_outs)
    ig0 = return_inputs(0, near_outs, inputs(0))
    both(hg, "relay", "get2")
    both(pre, "relay", "get2")

    both(hg, "wait", "get2")
    far_outs = outs(1)
    eo1 = return_outs(1, far_outs)

    both(pre, "wait", "get2")
    ig1 = return_inputs(1, far_outs, inputs(1))

    @pl.loop(0, SIDE)
    def _(q):
        left0, right0, _ = hidden_of(0, q)
        left1, right1, _ = hidden_of(1, q)
        hidden0 = jnp.concatenate([left0, right0], axis=1)
        hidden1 = jnp.concatenate([left1, right1], axis=1)
        woutg[span(q, quarter), :] = (dot(hidden0, gs[0], 0, 0) + dot(hidden1, gs[1], 0, 0)).astype(BF)

    store_out = pltpu.make_async_copy(woutg, woutg_hbm, local.at[2])
    store_out.start()


    for part in range(2):
        @pl.loop(0, SIDE)
        def _(q):
            wing[:, span(q, quarter, part * ff)] = (
                dot(xs[0], unit_of(0, part, q), 0, 0) + dot(xs[1], unit_of(1, part, q), 0, 0)).astype(BF)

    store_in = pltpu.make_async_copy(wing, wing_hbm, local.at[3])
    store_in.start()

    def parts(table, got, size, chunk):
        at = pl.ds(chunk * near * size, near * size)
        rows_ = got[pl.ds(chunk * near, near)].reshape(near * size, LANES)
        return [dot(table[at, pl.ds(i * LANES, LANES)], rows_, 0, 0) for i in range(4)]

    eo0.wait()
    ig0.wait()
    ends = parts(back1, e1, one, 0)
    sides = parts(back2, e2, two, 0)
    eo1.wait()
    sides = [x + y for x, y in zip(sides, parts(back2, e2, two, 1))]
    ig1.wait()
    ends = [x + y for x, y in zip(ends, parts(back1, e1, one, 1))]
    out[...] = jnp.concatenate([sides[0] + sides[1], sides[2] + sides[3] + ends[2] + ends[3]], axis=1).astype(BF)
    tgrad[...] = jnp.concatenate([ends[0], ends[1]], axis=1).astype(BF)
    store_out.wait()
    store_in.wait()


def kernel(peers, cap, *refs):
    started = []
    steps(peers, cap, *refs, started)
    for move in started:
        if not move.arrived:
            move.wait()
    for move in started:
        move.leave()


def finish(parts, *refs):
    srcs, dsts, holds, ins, outs = refs[:4], refs[4:8], refs[8:12], refs[12], refs[13]
    ways = []
    for src, dst, hold, cuts in zip(srcs, dsts, holds, parts):
        step = src.shape[0] // cuts
        for i in range(cuts):
            at, n = pl.ds(i * step, step), len(ways)
            ways.append((pltpu.make_async_copy(src.at[at], hold.at[at], ins.at[n]),
                         pltpu.make_async_copy(hold.at[at], dst.at[at], outs.at[n])))
    for load, _ in ways:
        load.start()
    for load, store in ways:
        load.wait()
        store.start()
    for _, store in ways:
        store.wait()


def body(tokens, expert_ids, gate_codes, out_grad, w_in, w_out):
    peers = lax.axis_size("expert")
    count, width = tokens.shape
    top = expert_ids.shape[1]
    ff = w_out.shape[1]
    cap = 3 * count * top // (2 * ALL_EXP)
    rows = cap * peers // 2
    height, quarter = rows // SIDE, ff // SIDE
    one, two = 32, 16
    vm = lambda *shape: pltpu.VMEM(shape, BF)
    widths = (quarter + 256, quarter + 128, quarter, quarter, 128, 256)
    m1, m2 = vm(peers, one, LANES), vm(peers, two, LANES)
    scratch = [
        vm(width, 2 * ff), vm(ff, width), vm(width, 2 * ff), vm(ff, width),
        m1, m2, m1, m2, m1, m2, m1, m2,
        vm(2, rows, width), vm(2, rows, width),
        vm(peers * one, 4 * count), vm(peers * two, 4 * count),
        vm(3, rows, peers // 2 * one), vm(3, peers // 2 * one, rows),
        vm(2, rows, peers // 2 * two), vm(2, peers // 2 * two, rows),
        [vm(SIDE, height, SIDE * w) for w in widths],
        [vm(SIDE, height, SIDE * w) for w in widths],
        [Half.scratch(i % 2 == 0, height, w) for i, w in enumerate(widths)],
        pltpu.SemaphoreType.DMA((144,)), pltpu.SemaphoreType.DMA((144,)),
        pltpu.SemaphoreType.DMA((8,)), pltpu.SemaphoreType.DMA((8,)), pltpu.SemaphoreType.DMA((4,)),
    ]
    vmem, hbm = pl.BlockSpec(memory_space=pltpu.VMEM), pl.BlockSpec(memory_space=pl.ANY)
    shapes = (
        jax.ShapeDtypeStruct((count, width), BF), jax.ShapeDtypeStruct((count, width), BF),
        jax.ShapeDtypeStruct((width, 2 * ff), BF), jax.ShapeDtypeStruct((ff, width), BF))
    results = pl.pallas_call(
        functools.partial(kernel, peers, cap),
        out_shape=shapes,
        in_specs=[vmem, vmem, vmem, vmem, hbm, hbm],
        out_specs=(vmem, vmem, hbm, hbm),
        scratch_shapes=scratch,
        compiler_params=pltpu.CompilerParams(
            collective_id=0, has_side_effects=True, vmem_limit_bytes=40 * 1024 * 1024),
        cost_estimate=pl.CostEstimate(
            flops=4 * rows * width * ff * 9, bytes_accessed=12 * width * ff, transcendentals=rows * quarter),
    )(tokens, expert_ids.T, gate_codes.T, out_grad, w_in[0], w_out[0])
    out, tgrad, wing, woutg = pl.pallas_call(
        functools.partial(finish, (1, 1, 4, 2)),
        out_shape=shapes,
        in_specs=[hbm] * 4,
        out_specs=(hbm,) * 4,
        scratch_shapes=[pltpu.VMEM(s.shape, BF) for s in shapes] + [pltpu.SemaphoreType.DMA((8,))] * 2,
    )(*results)
    return out, tgrad, wing[None], woutg[None]


def solution(mesh):
    placed = (
        P("expert", "dp"),
        P("expert", None),
        P("expert", None),
        P("expert", "dp"),
        P("expert", "dp", None),
        P("expert", None, "dp"),
    )
    return jax.shard_map(
        body,
        mesh=mesh,
        in_specs=placed,
        out_specs=(
            P("expert", "dp"),
            P("expert", "dp"),
            P("expert", "dp", None),
            P("expert", None, "dp"),
        ),
        check_vma=False,
    )
```
